32 devices in a mesh: groups: 2 (over y), region: 4 (over z), sub: 2 (over x), lane: 2 (over core).
Axes of the slice: x: 2, y: 2, z: 4, core: 2. Of those that a mesh axis runs over, the one named last changes fastest.
Arguments:
- features: bfloat16 [32, 16, 16, 1024], P(None, 'sub', 'lane', ('groups', 'region')), parts along dimension 3, may hold values from -6 to 6
- occupancy: int32 [16, 16, 1024], P('sub', 'lane', ('groups', 'region')), parts along dimension 2, may hold values 0 or 1
- brick_list: int32 [8, 2, 2, 8], P(('groups', 'region'), 'sub', 'lane'), parts along dimension 0, may hold values from 0 to 15, as said below
- brick_count: int32 [8, 2, 2], P(('groups', 'region'), 'sub', 'lane'), parts along dimension 0, may hold values from 0 to 8, as said below
- weight_one: bfloat16 [27, 32, 32], replicated, may hold values from -0.21875 to 0.21875
- scale_one: float32 [32], replicated, may hold values from 0.25 to 1.75
- shift_one: float32 [32], replicated, may hold values from -3 to 3
- weight_two: bfloat16 [27, 32, 32], replicated, may hold values from -0.21875 to 0.21875
- scale_two: float32 [32], replicated, may hold values from 0.25 to 1.75
- shift_two: float32 [32], replicated, may hold values from -3 to 3
Outputs:
- output: bfloat16 [32, 16, 16, 1024], P(None, 'sub', 'lane', ('groups', 'region')), parts along dimension 3
The draws below stay inside these ranges and needn't reach their ends.
There are 2 independent parts, one for each index of `groups`. The reference program is written for one: setup_inputs(seed, part) draws one part's arguments, and reference() takes and returns one part's arrays. A program takes and returns all parts, laid end to end along the dimension named above; an argument that names none is the same for every part. Nothing has to cross between parts.
Inputs may be any that keep to these rules, and one draw needn't show every extreme that they name: `brick_count`: no device has more than 8 active bricks, and the counts of the two devices whose region indices differ by 4 / 2 (same sub and lane) sum to at most 8; some device has exactly 8. `brick_list`: each device's list holds distinct slot numbers; entries at or after the device's count are not live.
All inputs are finite; a program needn't handle non-finite values. No bound on the sum of `occupancy` on one device may be relied on, other than what follows from the above.
Results may differ from the reference program's by a relative error of at most 0.006.
Values may be sent and summed in bfloat16 or wider, within the bound.
A program may use at most 64 MiB of HBM per device.

```python
import jax
import jax.numpy as jnp
from jax import lax

C = 32
BY_DEV = 1
BZ_DEV = 16
SLOTS = 16
CAP = 8
GX = 16
GY = 16
GZ = 512
N_REGION = 4
N_SUB = 2
N_LANE = 2


def draw_brick_count(key, part):
    key = jax.random.fold_in(key, 11)
    first_key, second_key = jax.random.split(key)
    half = N_REGION // 2
    totals = jax.random.randint(first_key, (half, N_SUB, N_LANE), CAP // 4, CAP + 1)
    first = jax.random.randint(second_key, (half, N_SUB, N_LANE), 0, totals + 1)
    counts = jnp.concatenate([first, totals - first], axis=0)
    counts = counts.at[0, 0, 0].set(CAP).at[half, 0, 0].set(0)
    return counts.astype(jnp.int32)


def draw_brick_list(key, part):
    key = jax.random.fold_in(key, 23)
    keys = jax.random.split(key, N_REGION * N_SUB * N_LANE)
    orders = jax.vmap(lambda k: jax.random.permutation(k, SLOTS))(keys)[:, :CAP]
    return orders.reshape(N_REGION, N_SUB, N_LANE, CAP).astype(jnp.int32)


def place_ends(array, rng, low, high):
    longest = array.shape.index(max(array.shape))
    spots = []
    for shift in (0, 1):
        where = [jax.random.randint(jax.random.fold_in(rng, axis), (), 0, length) for axis, length in enumerate(array.shape)]
        where[longest] = (where[longest] + shift) % array.shape[longest]
        spots.append(tuple(where))
    return array.at[spots[0]].set(low).at[spots[1]].set(high)


def level_of(stream_key, extent, shards, smallest, largest):
    level, own = 1.0, jax.random.fold_in(stream_key, 6)
    for axis_at, shards_of in shards:
        draws = jnp.exp(jax.random.uniform(jax.random.fold_in(own, axis_at), (shards_of,), jnp.float32, smallest / len(shards), largest / len(shards)))
        level = level * jnp.repeat(draws, extent[axis_at] // shards_of).reshape([-1 if axis == axis_at else 1 for axis in range(len(extent))])
    return level


def scatter_about(rng, dims, spread, limit, cuts=(), kind=jnp.bfloat16):
    loudness = level_of(rng, dims, cuts, -0.22, 0.18) if cuts else 1.0
    drawn = jax.random.normal(rng, dims, jnp.float32) * spread * loudness
    return jnp.minimum(jnp.maximum(drawn, -limit), limit).astype(kind)


def setup_inputs(seed: int = 0, part: int = 0) -> dict:
    streams_of = jax.random.split(jax.random.key(seed), 11)
    part_keys = jax.random.split(jax.random.fold_in(streams_of[10], part), 11)
    features = scatter_about(part_keys[0], (C, GX, GY, GZ), 1.0, 6.0, ((1, 2), (2, 2), (3, 4)))
    occupancy = place_ends((jax.random.randint(part_keys[1], (GX, GY, GZ), 0, 5) < 3).astype(jnp.int32), jax.random.fold_in(part_keys[1], 1), 0, 1)
    brick_list = draw_brick_list(jax.random.fold_in(jax.random.fold_in(streams_of[10], part), 71), part)
    brick_count = draw_brick_count(jax.random.fold_in(jax.random.fold_in(streams_of[10], part), 71), part)
    weight_one = scatter_about(streams_of[4], (27, C, C), (27 * C) ** -0.5, 0.21875)
    scale_one = jnp.clip(1.0 + 0.15 * jax.random.normal(streams_of[5], (C,), jnp.float32), 0.25, 1.75)
    shift_one = scatter_about(streams_of[6], (C,), 0.5, 3.0, (), jnp.float32)
    weight_two = scatter_about(streams_of[7], (27, C, C), (27 * C) ** -0.5, 0.21875)
    scale_two = jnp.clip(1.0 + 0.15 * jax.random.normal(streams_of[8], (C,), jnp.float32), 0.25, 1.75)
    shift_two = scatter_about(streams_of[9], (C,), 0.5, 3.0, (), jnp.float32)
    return {"features": features, "occupancy": occupancy, "brick_list": brick_list, "brick_count": brick_count, "weight_one": weight_one, "scale_one": scale_one, "shift_one": shift_one, "weight_two": weight_two, "scale_two": scale_two, "shift_two": shift_two}


def convolve(field, weight):
    kernel = weight.astype(jnp.float32).reshape(3, 3, 3, C, C).transpose(3, 4, 0, 1, 2)
    result = lax.conv_general_dilated(field[None], kernel, (1, 1, 1), ((1, 1), (1, 1), (1, 1)), precision=lax.Precision.HIGHEST)
    return result[0]


def live_voxels(occupancy, brick_list, brick_count):
    slot_ids = jnp.arange(SLOTS, dtype=jnp.int32)
    valid = jnp.arange(CAP, dtype=jnp.int32) < brick_count[..., None]
    hits = (brick_list[..., None] == slot_ids) & valid[..., None]
    live = jnp.any(hits, axis=3)
    live = live.reshape(N_REGION, N_SUB, N_LANE, BY_DEV, BZ_DEV).transpose(1, 2, 3, 0, 4)
    live = live.reshape(N_SUB, N_LANE * BY_DEV, N_REGION * BZ_DEV)
    live = jnp.repeat(jnp.repeat(jnp.repeat(live, 8, 0), 8, 1), 8, 2)
    return (occupancy == 1) & live


def reference(features, occupancy, brick_list, brick_count, weight_one, scale_one, shift_one, weight_two, scale_two, shift_two):
    active = live_voxels(occupancy, brick_list, brick_count).astype(jnp.float32)
    start = (features.astype(jnp.float32) * active).astype(jnp.bfloat16)
    first_sum = convolve(start.astype(jnp.float32), weight_one)
    first = (active * jax.nn.relu(first_sum * scale_one[:, None, None, None] + shift_one[:, None, None, None])).astype(jnp.bfloat16)
    second_sum = convolve(first.astype(jnp.float32), weight_two)
    second = (active * jax.nn.relu(second_sum * scale_two[:, None, None, None] + shift_two[:, None, None, None])).astype(jnp.bfloat16)
    return (active * (second.astype(jnp.float32) + start.astype(jnp.float32))).astype(jnp.bfloat16)
```

```python
import functools

import jax
import jax.numpy as jnp
from jax import lax
from jax.experimental import pallas as pl
from jax.experimental.pallas import tpu as pltpu
from jax.sharding import PartitionSpec as P

BF = jnp.bfloat16
F32 = jnp.float32
MESH = pl.DeviceIdType.MESH

KINDS = [
    (dr, ds, dl) for dr in (0, -1, 1) for ds in (0, -1, 1) for dl in (0, 1) if (dr, ds, dl) != (0, 0, 0)
]


def dot(a, b):
    return jnp.dot(a, b, preferred_element_type=F32)


def dot_nt(a, b):
    return lax.dot_general(a, b, (((1,), (1,)), ((), ())), preferred_element_type=F32)


def iota(shape, dim):
    return lax.broadcasted_iota(jnp.int32, shape, dim)


def onehot(cond):
    return jnp.where(cond, 1.0, 0.0).astype(BF)


def kernel(
    n_region, n_sub,
    feat, occ, bricks, count, w1, s1, h1, w2, s2, h2, out,
    D, DY, B, BY, BC, WC, ACC, G, ACT, SX, SY, SZ, RX, RY, RZ, send_sem, recv_sem,
):
    r = lax.axis_index("region")
    s = lax.axis_index("sub")
    l = lax.axis_index("lane")
    edge = 7 * (1 - l)
    far = 7 * l

    def inside(dr, ds):
        a, b = r + dr, s + ds
        return (a >= 0) & (a < n_region) & (b >= 0) & (b < n_sub)

    def target(dr, ds, dl):
        return {"region": r + dr, "sub": s + ds, "lane": 1 - l if dl else l}

    barrier = pltpu.get_barrier_semaphore()
    RX[...] = jnp.zeros_like(RX)
    RY[...] = jnp.zeros_like(RY)
    RZ[...] = jnp.zeros_like(RZ)
    for kind in KINDS:
        @pl.when(inside(kind[0], kind[1]))
        def _(kind=kind):
            pl.semaphore_signal(barrier, inc=1, device_id=target(*kind), device_id_type=MESH)

    def message(rnd, k):
        dr, ds, dl = KINDS[k]
        if dr:
            src = SZ.at[rnd]
            dst = RZ.at[rnd, dl, pl.ds((0 if dr == 1 else 48) + (1 - ds) * 16, 16)]
        elif not dl:
            src = SX.at[rnd, 0 if ds == -1 else 1]
            dst = RX.at[rnd, 1 if ds == -1 else 0]
        elif ds == 0:
            src = SY.at[rnd]
            dst = RY.at[rnd, pl.ds(32, 256)]
        else:
            src = SY.at[rnd, pl.ds(0 if ds == -1 else 224, 32)]
            dst = RY.at[rnd, pl.ds(288 if ds == -1 else 0, 32)]
        return pltpu.make_async_remote_copy(
            src_ref=src, dst_ref=dst, send_sem=send_sem.at[rnd, k], recv_sem=recv_sem.at[rnd, k],
            device_id=target(dr, ds, dl), device_id_type=MESH,
        )

    def send(rnd):
        for k, (dr, ds, dl) in enumerate(KINDS):
            @pl.when(inside(dr, ds))
            def _(k=k):
                message(rnd, k).start()

    def arrived(rnd):
        for k, (dr, ds, dl) in enumerate(KINDS):
            @pl.when(inside(-dr, -ds))
            def _(k=k):
                message(rnd, k).wait_recv()

    def sent(rnd):
        for k, (dr, ds, dl) in enumerate(KINDS):
            @pl.when(inside(dr, ds))
            def _(k=k):
                message(rnd, k).wait_send()

    lane128 = iota((8, 128), 1)
    slot = lane128 >> 3
    live = jnp.zeros((8, 128), F32)
    n_live = count[0, 0, 0]
    for k in range(bricks.shape[3]):
        entry = jnp.where(k < n_live, bricks[0, 0, 0, k], -1)
        live = jnp.where(slot == entry, 1.0, live)
    for x in range(8):
        ACT[x] = jnp.where(occ[x] == 1, live, 0.0)

    zl = iota((256, 128), 1)

    def shifted(v):
        before = jnp.where(zl[: v.shape[0]] == 0, 0.0, pltpu.roll(v, 1, 1))
        after = jnp.where(zl[: v.shape[0]] == 127, 0.0, pltpu.roll(v, 127, 1))
        return before.astype(BF), v.astype(BF), after.astype(BF)

    def places(x):
        got = []
        if -1 <= x <= 4:
            got.append((x + 1, 0))
        if 3 <= x <= 8:
            got.append((x - 3, 1))
        return got

    def put_plane(rnd, x, v):
        three = shifted(v)
        for p, h in places(x):
            for dz in range(3):
                D[rnd, p, dz, :, pl.ds(h * 128, 128)] = three[dz]
        if x == 0:
            SX[rnd, 0] = three[1]
        if x == 7:
            SX[rnd, 1] = three[1]

    ci = iota((32, 256), 0)
    cj = iota((32, 256), 1)
    spread = onehot(ci == (cj >> 3))
    pick_edge = onehot((ci == (cj >> 3)) & ((cj & 7) == edge))
    e_row = iota((16, 128), 0)
    e_lane = iota((16, 128), 1)

    def pack(rnd):
        columns = jnp.zeros((16, 256), F32)
        for x in range(8):
            p, h = places(x)[0]
            take = onehot(((e_row == x) & (e_lane == 0)) | ((e_row == 8 + x) & (e_lane == 127)))
            v = D[rnd, p, 1, :, pl.ds(h * 128, 128)]
            columns += dot_nt(take, v)
            SY[rnd, pl.ds(x * 32, 32)] = dot(pick_edge, v).astype(BF)
        SZ[rnd] = columns.astype(BF)

    for x in range(8):
        v = feat[:, x].astype(F32) * ACT[x][None]
        put_plane(0, x, v.reshape(256, 128))
    pack(0)
    def span(at, size):
        return 1 + jnp.where(at > 0, 1, 0) + jnp.where(at < size - 1, 1, 0)

    pl.semaphore_wait(barrier, span(r, n_region) * span(s, n_sub) * 2 - 1)
    send(0)

    ri = iota((256, 256), 0)
    rj = iota((256, 256), 1)
    order = onehot((ri >> 3 == (rj & 31)) & ((ri & 7) == (rj >> 5)))
    bi = iota((256, 32), 0)
    bj = iota((256, 32), 1)
    put_edge = onehot(((bi >> 3) == bj) & ((bi & 7) == edge))
    band = [onehot((cj & 7) == k) for k in range(8)]
    far_band = onehot((cj & 7) == far)

    def build(layer, w):
        WC[...] = dot(w[...].reshape(27 * 32, 32), spread).astype(BF)
        for dx in range(3):
            for dz in range(3):
                taps = [WC[pl.ds((9 * dx + 3 * dy + dz) * 32, 32)] for dy in range(3)]
                blocks = []
                for y in range(8):
                    block = taps[1] * band[y]
                    if y > 0:
                        block = block + taps[0] * band[y - 1]
                    if y < 7:
                        block = block + taps[2] * band[y + 1]
                    blocks.append(block)
                full = jnp.concatenate(blocks, axis=0)
                B[layer, :, pl.ds((dx * 3 + dz) * 256, 256)] = dot(order, full).astype(BF)
                if dz != 1:
                    start = pl.multiple_of((9 * dx + 3 * (2 - 2 * l) + dz) * 32, 32)
                    BC[layer, dx * 2 + dz // 2] = dot(put_edge, WC[pl.ds(start, 32)] * far_band).astype(BF)
        side = jnp.zeros((32, 288), F32)
        pi = iota((32, 288), 0)
        pj = iota((32, 288), 1)
        for dx in range(3):
            for dz in range(3):
                tap = w[9 * dx + 3 * (2 - 2 * l) + dz]
                side += dot(tap, onehot(pj == pi + 32 * (dx * 3 + dz)))
        BY[layer] = dot(put_edge, side.astype(BF)).astype(BF)

    build(0, w1)
    build(1, w2)

    si = iota((96, 96), 0)
    sj = iota((96, 96), 1)
    q, j = si >> 4, si & 15
    plus = q & 1
    e = (j >> 1) + (q >> 1) + 7
    source = plus * 48 + (e >> 3) * 16 + (1 - plus) * 8 + (e & 7)
    place = onehot((sj == source) & ((j & 1) == 1 - plus))

    def rows_of(ref):
        own = jnp.broadcast_to(ref[...], (256, 32))
        return jnp.sum(jnp.where((bi >> 3) == bj, own, 0.0), axis=1, keepdims=True)

    G[...] = jnp.zeros_like(G)

    def main(layer, xx):
        return dot(B[layer], D[layer, pl.ds(xx, 3)].reshape(2304, 256))

    def layer_sums(layer):
        for xx in (1, 2):
            ACC[xx] = main(layer, xx)
        arrived(layer)
        for x, side in ((-1, 0), (8, 1)):
            put_plane(layer, x, RX[layer, side].astype(F32))
        for x in range(-1, 9):
            three = shifted(RY[layer, pl.ds((x + 1) * 32, 32)].astype(F32))
            for p, h in places(x):
                for dz in range(3):
                    DY[layer, pl.ds(p * 96 + dz * 32, 32), pl.ds(h * 128, 128)] = three[dz]
        own = dot(place, RZ[layer, 0]).astype(BF)
        other = dot(place, RZ[layer, 1]).astype(BF)
        total = jnp.zeros((256, 16), F32)
        for q in range(6):
            dx, dz = q // 2, 2 * (q % 2)
            total += dot_nt(B[layer, :, pl.ds((dx * 3 + dz) * 256, 256)], own[q * 16 : q * 16 + 16])
            total += dot_nt(BC[layer, q], other[q * 16 : q * 16 + 16])
        G[:, pl.ds(0, 16)] = total

    ends = (zl == 0) | (zl == 127)

    def finish(layer, xx, scale, shift):
        acc = ACC[xx] if xx in (1, 2) else main(layer, xx)
        acc = acc + dot(BY[layer], DY[layer, pl.ds(xx * 96, 288)])
        got = []
        for h in range(2):
            x = xx + 4 * h
            v = acc[:, h * 128 : h * 128 + 128]
            v = v + jnp.where(ends, pltpu.roll(G[...], 128 - (2 * x + 1), 1), 0.0)
            v = jnp.maximum(v * scale + shift, 0.0).reshape(32, 8, 128) * ACT[x][None]
            got.append((x, v))
        return got

    layer_sums(0)
    scale, shift = rows_of(s1), rows_of(h1)
    for xx in (0, 3, 1, 2):
        for x, v in finish(0, xx, scale, shift):
            put_plane(1, x, v.reshape(256, 128).astype(BF).astype(F32))
    pack(1)
    send(1)

    layer_sums(1)
    scale, shift = rows_of(s2), rows_of(h2)
    for xx in (1, 2, 0, 3):
        for x, v in finish(1, xx, scale, shift):
            p, h = places(x)[0]
            begin = D[0, p, 1, :, pl.ds(h * 128, 128)].astype(F32).reshape(32, 8, 128)
            v = (v.astype(BF).astype(F32) + begin) * ACT[x][None]
            out[:, x] = v.astype(BF)
    sent(0)
    sent(1)


def body(n_region, n_sub, features, occupancy, brick_list, brick_count, w1, s1, h1, w2, s2, h2):
    assert features.shape == (32, 8, 8, 128)
    vmem = pl.BlockSpec(memory_space=pltpu.VMEM)
    smem = pl.BlockSpec(memory_space=pltpu.SMEM)
    return pl.pallas_call(
        functools.partial(kernel, n_region, n_sub),
        out_shape=jax.ShapeDtypeStruct(features.shape, BF),
        in_specs=[vmem, vmem, smem, smem] + [vmem] * 6,
        out_specs=vmem,
        scratch_shapes=[
            pltpu.VMEM((2, 6, 3, 256, 256), BF),
            pltpu.VMEM((2, 576, 256), BF),
            pltpu.VMEM((2, 256, 2304), BF),
            pltpu.VMEM((2, 256, 288), BF),
            pltpu.VMEM((2, 6, 256, 256), BF),
            pltpu.VMEM((864, 256), BF),
            pltpu.VMEM((4, 256, 256), F32),
            pltpu.VMEM((256, 128), F32),
            pltpu.VMEM((8, 8, 128), F32),
            pltpu.VMEM((2, 2, 256, 128), BF),
            pltpu.VMEM((2, 256, 128), BF),
            pltpu.VMEM((2, 16, 256), BF),
            pltpu.VMEM((2, 2, 256, 128), BF),
            pltpu.VMEM((2, 320, 128), BF),
            pltpu.VMEM((2, 2, 96, 256), BF),
            pltpu.SemaphoreType.DMA((2, len(KINDS))),
            pltpu.SemaphoreType.DMA((2, len(KINDS))),
        ],
        compiler_params=pltpu.CompilerParams(
            collective_id=0, has_side_effects=True, vmem_limit_bytes=48 * 1024 * 1024
        ),
    )(features, occupancy, brick_list, brick_count, w1, s1.reshape(1, -1), h1.reshape(1, -1), w2, s2.reshape(1, -1), h2.reshape(1, -1))


def solution(mesh):
    assert mesh.shape["lane"] == 2
    placed = (
        P(None, "sub", "lane", ("groups", "region")),
        P("sub", "lane", ("groups", "region")),
        P(("groups", "region"), "sub", "lane", None),
        P(("groups", "region"), "sub", "lane"),
        P(), P(), P(), P(), P(), P(),
    )
    return jax.shard_map(
        functools.partial(body, mesh.shape["region"], mesh.shape["sub"]),
        mesh=mesh,
        in_specs=placed,
        out_specs=P(None, "sub", "lane", ("groups", "region")),
        check_vma=False,
    )
```

```python
import functools

import jax
import jax.numpy as jnp
from jax import lax
from jax.experimental import pallas as pl
from jax.experimental.pallas import tpu as pltpu
from jax.sharding import PartitionSpec as P

BF = jnp.bfloat16
F32 = jnp.float32
MESH = pl.DeviceIdType.MESH

KINDS = [
    (dr, ds, dl) for dr in (0, -1, 1) for ds in (0, -1, 1) for dl in (0, 1) if (dr, ds, dl) != (0, 0, 0)
]


def dot(a, b):
    return jnp.dot(a, b, preferred_element_type=F32)


def dot_nt(a, b):
    return lax.dot_general(a, b, (((1,), (1,)), ((), ())), preferred_element_type=F32)


def iota(shape, dim):
    return lax.broadcasted_iota(jnp.int32, shape, dim)


def onehot(cond):
    return jnp.where(cond, 1.0, 0.0).astype(BF)


def kernel(
    n_region, n_sub,
    feat_hbm, occ_hbm, bricks_hbm, count_hbm, w1_hbm, s1_hbm, h1_hbm, w2_hbm, s2_hbm, h2_hbm, out,
    feat, occ, bricks, count, w1, s1, h1, w2, s2, h2, load_sem, DX, D, DY, B, BY, BC, WC, ACC, G, ACT, SX, SY, SZ, RX, RY, RZ, send_sem, recv_sem,
):
    r = lax.axis_index("region")
    s = lax.axis_index("sub")
    l = lax.axis_index("lane")
    edge = 7 * (1 - l)
    far = 7 * l

    def inside(dr, ds):
        a, b = r + dr, s + ds
        return (a >= 0) & (a < n_region) & (b >= 0) & (b < n_sub)

    def target(dr, ds, dl):
        return {"region": r + dr, "sub": s + ds, "lane": 1 - l if dl else l}

    pairs = [
        (count_hbm, count), (bricks_hbm, bricks), (occ_hbm, occ), (feat_hbm, feat), (w1_hbm, w1), (w2_hbm, w2),
        (s1_hbm, s1), (h1_hbm, h1), (s2_hbm, s2), (h2_hbm, h2),
    ]
    loads = [pltpu.make_async_copy(a, b, load_sem.at[i]) for i, (a, b) in enumerate(pairs)]
    for load in loads:
        load.start()
    barrier = pltpu.get_barrier_semaphore()
    RX[...] = jnp.zeros_like(RX)
    for rnd in range(2):
        D[rnd, 0, :, :, pl.ds(0, 128)] = jnp.zeros((3, 256, 128), BF)
        D[rnd, 5, :, :, pl.ds(128, 128)] = jnp.zeros((3, 256, 128), BF)
    RY[...] = jnp.zeros_like(RY)
    RZ[...] = jnp.zeros_like(RZ)
    for kind in KINDS:
        @pl.when(inside(kind[0], kind[1]))
        def _(kind=kind):
            pl.semaphore_signal(barrier, inc=1, device_id=target(*kind), device_id_type=MESH)

    def message(rnd, k):
        dr, ds, dl = KINDS[k]
        if dr:
            src = SZ.at[rnd]
            dst = RZ.at[rnd, dl, pl.ds((0 if dr == 1 else 48) + (1 - ds) * 16, 16)]
        elif not dl:
            src = SX.at[rnd, 0 if ds == -1 else 1]
            dst = RX.at[rnd, 1 if ds == -1 else 0]
        elif ds == 0:
            src = SY.at[rnd]
            dst = RY.at[rnd, pl.ds(32, 256)]
        else:
            src = SY.at[rnd, pl.ds(0 if ds == -1 else 224, 32)]
            dst = RY.at[rnd, pl.ds(288 if ds == -1 else 0, 32)]
        return pltpu.make_async_remote_copy(
            src_ref=src, dst_ref=dst, send_sem=send_sem.at[rnd, k], recv_sem=recv_sem.at[rnd, k],
            device_id=target(dr, ds, dl), device_id_type=MESH,
        )

    def group(kind):
        dr, ds, dl = kind
        return "z" if dr else "x" if not dl else "edge" if ds else "y"

    def send(rnd, which):
        for k, (dr, ds, dl) in enumerate(KINDS):
            if group(KINDS[k]) in which:
                @pl.when(inside(dr, ds))
                def _(k=k):
                    message(rnd, k).start()

    def arrived(rnd, which):
        for k, (dr, ds, dl) in enumerate(KINDS):
            if group(KINDS[k]) in which:
                @pl.when(inside(-dr, -ds))
                def _(k=k):
                    message(rnd, k).wait_recv()

    def sent(rnd):
        for k, (dr, ds, dl) in enumerate(KINDS):
            @pl.when(inside(dr, ds))
            def _(k=k):
                message(rnd, k).wait_send()

    for load in loads[:4]:
        load.wait()
    lane128 = iota((8, 128), 1)
    slot = lane128 >> 3
    live = jnp.zeros((8, 128), F32)
    n_live = count[0, 0, 0]
    for k in range(bricks.shape[3]):
        entry = jnp.where(k < n_live, bricks[0, 0, 0, k], -1)
        live = jnp.where(slot == entry, 1.0, live)
    for x in range(8):
        ACT[x] = jnp.where(occ[x] == 1, live, 0.0)

    zl = iota((256, 128), 1)

    def shifted(v):
        before = jnp.where(zl[: v.shape[0]] == 0, 0.0, pltpu.roll(v, 1, 1))
        after = jnp.where(zl[: v.shape[0]] == 127, 0.0, pltpu.roll(v, 127, 1))
        return before.astype(BF), v.astype(BF), after.astype(BF)

    def places(x):
        got = []
        if -1 <= x <= 4:
            got.append((x + 1, 0))
        if 3 <= x <= 8:
            got.append((x - 3, 1))
        return got

    def put_plane(rnd, x, v):
        three = shifted(v)
        for p, h in places(x):
            for dz in range(3):
                D[rnd, p, dz, :, pl.ds(h * 128, 128)] = three[dz]
        if x == 0:
            SX[rnd, 0] = three[1]
        if x == 7:
            SX[rnd, 1] = three[1]

    ci = iota((32, 256), 0)
    cj = iota((32, 256), 1)
    spread = onehot(ci == (cj >> 3))
    pick_edge = onehot((ci == (cj >> 3)) & ((cj & 7) == edge))
    e_row = iota((16, 128), 0)
    e_lane = iota((16, 128), 1)

    def pack(rnd):
        columns = jnp.zeros((16, 256), F32)
        for x in range(8):
            p, h = places(x)[0]
            take = onehot(((e_row == x) & (e_lane == 0)) | ((e_row == 8 + x) & (e_lane == 127)))
            v = D[rnd, p, 1, :, pl.ds(h * 128, 128)]
            columns += dot_nt(take, v)
            SY[rnd, pl.ds(x * 32, 32)] = dot(pick_edge, v).astype(BF)
        SZ[rnd] = columns.astype(BF)

    def span(at, size):
        return 1 + jnp.where(at > 0, 1, 0) + jnp.where(at < size - 1, 1, 0)

    for x in (0, 7, 1, 2, 3, 4, 5, 6):
        v = feat[:, x].astype(F32) * ACT[x][None]
        put_plane(0, x, v.reshape(256, 128))
    pack(0)
    pl.semaphore_wait(barrier, span(r, n_region) * span(s, n_sub) * 2 - 1)
    send(0, ("z",))
    send(0, ("x",))
    send(0, ("edge", "y"))

    ri = iota((256, 256), 0)
    rj = iota((256, 256), 1)
    order = onehot((ri >> 3 == (rj & 31)) & ((ri & 7) == (rj >> 5)))
    bi = iota((256, 32), 0)
    bj = iota((256, 32), 1)
    put_edge = onehot(((bi >> 3) == bj) & ((bi & 7) == edge))
    band = [onehot((cj & 7) == k) for k in range(8)]
    far_band = onehot((cj & 7) == far)

    def build(layer, w):
        WC[...] = dot(w[...].reshape(27 * 32, 32), spread).astype(BF)
        for dx in range(3):
            for dz in range(3):
                taps = [WC[pl.ds((9 * dx + 3 * dy + dz) * 32, 32)] for dy in range(3)]
                blocks = []
                for y in range(8):
                    block = taps[1] * band[y]
                    if y > 0:
                        block = block + taps[0] * band[y - 1]
                    if y < 7:
                        block = block + taps[2] * band[y + 1]
                    blocks.append(block)
                full = jnp.concatenate(blocks, axis=0)
                B[layer, :, pl.ds((dx * 3 + dz) * 256, 256)] = dot(order, full).astype(BF)
                if dz != 1:
                    start = pl.multiple_of((9 * dx + 3 * (2 - 2 * l) + dz) * 32, 32)
                    BC[layer, dx * 2 + dz // 2] = dot(put_edge, WC[pl.ds(start, 32)] * far_band).astype(BF)
        side = jnp.zeros((32, 288), F32)
        pi = iota((32, 288), 0)
        pj = iota((32, 288), 1)
        for dx in range(3):
            for dz in range(3):
                tap = w[9 * dx + 3 * (2 - 2 * l) + dz]
                side += dot(tap, onehot(pj == pi + 32 * (dx * 3 + dz)))
        BY[layer] = dot(put_edge, side.astype(BF)).astype(BF)

    for load in loads[4:]:
        load.wait()
    build(0, w1)

    si = iota((96, 96), 0)
    sj = iota((96, 96), 1)
    q, j = si >> 4, si & 15
    plus = q & 1
    e = (j >> 1) + (q >> 1) + 7
    source = plus * 48 + (e >> 3) * 16 + (1 - plus) * 8 + (e & 7)
    place = onehot((sj == source) & ((j & 1) == 1 - plus))

    def rows_of(ref):
        own = jnp.broadcast_to(ref[...], (256, 32))
        return jnp.sum(jnp.where((bi >> 3) == bj, own, 0.0), axis=1, keepdims=True)

    G[...] = jnp.zeros_like(G)

    def main(layer, xx):
        return dot(B[layer], D[layer, pl.ds(xx, 3)].reshape(2304, 256))

    def put_rows(layer, x):
        three = shifted(RY[layer, pl.ds((x + 1) * 32, 32)].astype(F32))
        for p, h in places(x):
            for dz in range(3):
                DY[layer, pl.ds(p * 96 + dz * 32, 32), pl.ds(h * 128, 128)] = three[dz]

    def add_rows(layer, xx):
        ACC[xx] += dot(BY[layer], DY[layer, pl.ds(xx * 96, 288)])

    def layer_sums(layer):
        arrived(layer, ("y",))
        for x in range(8):
            put_rows(layer, x)
        add_rows(layer, 1)
        add_rows(layer, 2)
        arrived(layer, ("x",))
        for side, xx, first_row in ((0, 0, 0), (1, 3, 1536)):
            three = shifted(RX[layer, side].astype(F32))
            for dz in range(3):
                DX[side, dz] = three[dz]
            ACC[xx, :, pl.ds(side * 128, 128)] += dot(
                B[layer, :, pl.ds(first_row, 768)], DX[side].reshape(768, 128)
            )
        arrived(layer, ("edge",))
        put_rows(layer, -1)
        put_rows(layer, 8)
        add_rows(layer, 0)
        add_rows(layer, 3)
        arrived(layer, ("z",))
        own = dot(place, RZ[layer, 0]).astype(BF)
        other = dot(place, RZ[layer, 1]).astype(BF)
        total = jnp.zeros((256, 16), F32)
        for q in range(6):
            dx, dz = q // 2, 2 * (q % 2)
            total += dot_nt(B[layer, :, pl.ds((dx * 3 + dz) * 256, 256)], own[q * 16 : q * 16 + 16])
            total += dot_nt(BC[layer, q], other[q * 16 : q * 16 + 16])
        G[:, pl.ds(0, 16)] = total

    ends = (zl == 0) | (zl == 127)

    def finish(layer, xx, scale, shift):
        acc = ACC[xx]
        got = []
        for h in range(2):
            x = xx + 4 * h
            v = acc[:, h * 128 : h * 128 + 128]
            v = v + jnp.where(ends, pltpu.roll(G[...], 128 - (2 * x + 1), 1), 0.0)
            v = jnp.maximum(v * scale + shift, 0.0).reshape(32, 8, 128) * ACT[x][None]
            got.append((x, v))
        return got

    for xx in range(4):
        ACC[xx] = main(0, xx)
    build(1, w2)
    layer_sums(0)
    scale, shift = rows_of(s1), rows_of(h1)
    for xx in (0, 3, 1, 2):
        for x, v in finish(0, xx, scale, shift):
            put_plane(1, x, v.reshape(256, 128).astype(BF).astype(F32))
        if xx == 3:
            send(1, ("x",))
    pack(1)
    send(1, ("z",))
    send(1, ("edge", "y"))

    for xx in range(4):
        ACC[xx] = main(1, xx)
    layer_sums(1)
    scale, shift = rows_of(s2), rows_of(h2)
    for xx in (1, 2, 0, 3):
        for x, v in finish(1, xx, scale, shift):
            p, h = places(x)[0]
            begin = D[0, p, 1, :, pl.ds(h * 128, 128)].astype(F32).reshape(32, 8, 128)
            v = (v.astype(BF).astype(F32) + begin) * ACT[x][None]
            out[:, x] = v.astype(BF)
    sent(0)
    sent(1)


def body(n_region, n_sub, features, occupancy, brick_list, brick_count, w1, s1, h1, w2, s2, h2):
    assert features.shape == (32, 8, 8, 128)
    vmem = pl.BlockSpec(memory_space=pltpu.VMEM)
    hbm = pl.BlockSpec(memory_space=pltpu.HBM)
    scales = [v.reshape(1, -1) for v in (s1, h1, s2, h2)]
    return pl.pallas_call(
        functools.partial(kernel, n_region, n_sub),
        out_shape=jax.ShapeDtypeStruct(features.shape, BF),
        in_specs=[hbm] * 10,
        out_specs=vmem,
        scratch_shapes=[
            pltpu.VMEM(features.shape, BF),
            pltpu.VMEM(occupancy.shape, jnp.int32),
            pltpu.SMEM(brick_list.shape, jnp.int32),
            pltpu.SMEM(brick_count.shape, jnp.int32),
            pltpu.VMEM(w1.shape, BF),
            pltpu.VMEM((1, 32), F32),
            pltpu.VMEM((1, 32), F32),
            pltpu.VMEM(w2.shape, BF),
            pltpu.VMEM((1, 32), F32),
            pltpu.VMEM((1, 32), F32),
            pltpu.SemaphoreType.DMA((10,)),
            pltpu.VMEM((2, 3, 256, 128), BF),
            pltpu.VMEM((2, 6, 3, 256, 256), BF),
            pltpu.VMEM((2, 576, 256), BF),
            pltpu.VMEM((2, 256, 2304), BF),
            pltpu.VMEM((2, 256, 288), BF),
            pltpu.VMEM((2, 6, 256, 256), BF),
            pltpu.VMEM((864, 256), BF),
            pltpu.VMEM((4, 256, 256), F32),
            pltpu.VMEM((256, 128), F32),
            pltpu.VMEM((8, 8, 128), F32),
            pltpu.VMEM((2, 2, 256, 128), BF),
            pltpu.VMEM((2, 256, 128), BF),
            pltpu.VMEM((2, 16, 256), BF),
            pltpu.VMEM((2, 2, 256, 128), BF),
            pltpu.VMEM((2, 320, 128), BF),
            pltpu.VMEM((2, 2, 96, 256), BF),
            pltpu.SemaphoreType.DMA((2, len(KINDS))),
            pltpu.SemaphoreType.DMA((2, len(KINDS))),
        ],
        compiler_params=pltpu.CompilerParams(
            collective_id=0, has_side_effects=True, vmem_limit_bytes=64000 * 1024
        ),
    )(features, occupancy, brick_list, brick_count, w1, scales[0], scales[1], w2, scales[2], scales[3])


def solution(mesh):
    assert mesh.shape["lane"] == 2
    placed = (
        P(None, "sub", "lane", ("groups", "region")),
        P("sub", "lane", ("groups", "region")),
        P(("groups", "region"), "sub", "lane", None),
        P(("groups", "region"), "sub", "lane"),
        P(), P(), P(), P(), P(), P(),
    )
    return jax.shard_map(
        functools.partial(body, mesh.shape["region"], mesh.shape["sub"]),
        mesh=mesh,
        in_specs=placed,
        out_specs=P(None, "sub", "lane", ("groups", "region")),
        check_vma=False,
    )
```

```python
import functools

import jax
import jax.numpy as jnp
from jax import lax
from jax.experimental import pallas as pl
from jax.experimental.pallas import tpu as pltpu
from jax.sharding import PartitionSpec as P

BF = jnp.bfloat16
F32 = jnp.float32
MESH = pl.DeviceIdType.MESH

KINDS = [
    (dr, ds, dl) for dr in (0, -1, 1) for ds in (0, -1, 1) for dl in (0, 1) if (dr, ds, dl) != (0, 0, 0)
]


def dot(a, b):
    return jnp.dot(a, b, preferred_element_type=F32)


def dot_nt(a, b):
    return lax.dot_general(a, b, (((1,), (1,)), ((), ())), preferred_element_type=F32)


def iota(shape, dim):
    return lax.broadcasted_iota(jnp.int32, shape, dim)


def onehot(cond):
    return jnp.where(cond, 1.0, 0.0).astype(BF)


def kernel(
    n_region, n_sub,
    feat_hbm, occ_hbm, bricks_hbm, count_hbm, w1_hbm, s1_hbm, h1_hbm, w2_hbm, s2_hbm, h2_hbm, out_hbm,
    feat, occ, bricks, count, w1, s1, h1, w2, s2, h2, load_sem, out, out_sem, DX, D, DY, B, BY, BC, WC, ACC, G, ACT, SX, SY, SZ, RX, RY, RZ, send_sem, recv_sem,
):
    r = lax.axis_index("region")
    s = lax.axis_index("sub")
    l = lax.axis_index("lane")
    edge = 7 * (1 - l)
    far = 7 * l

    def inside(dr, ds):
        a, b = r + dr, s + ds
        return (a >= 0) & (a < n_region) & (b >= 0) & (b < n_sub)

    def target(dr, ds, dl):
        return {"region": r + dr, "sub": s + ds, "lane": 1 - l if dl else l}

    pairs = [
        (count_hbm, count), (bricks_hbm, bricks), (occ_hbm, occ), (feat_hbm, feat), (w1_hbm, w1), (w2_hbm, w2),
        (s1_hbm, s1), (h1_hbm, h1), (s2_hbm, s2), (h2_hbm, h2),
    ]
    loads = [pltpu.make_async_copy(a, b, load_sem.at[i]) for i, (a, b) in enumerate(pairs)]
    for load in loads:
        load.start()
    barrier = pltpu.get_barrier_semaphore()
    RX[...] = jnp.zeros_like(RX)
    for rnd in range(2):
        D[rnd, 0, :, :, pl.ds(0, 128)] = jnp.zeros((3, 256, 128), BF)
        D[rnd, 5, :, :, pl.ds(128, 128)] = jnp.zeros((3, 256, 128), BF)
    RY[...] = jnp.zeros_like(RY)
    RZ[...] = jnp.zeros_like(RZ)
    for kind in KINDS:
        @pl.when(inside(kind[0], kind[1]))
        def _(kind=kind):
            pl.semaphore_signal(barrier, inc=1, device_id=target(*kind), device_id_type=MESH)

    def message(rnd, k):
        dr, ds, dl = KINDS[k]
        if dr:
            src = SZ.at[rnd]
            dst = RZ.at[rnd, dl, pl.ds((0 if dr == 1 else 48) + (1 - ds) * 16, 16)]
        elif not dl:
            src = SX.at[rnd, 0 if ds == -1 else 1]
            dst = RX.at[rnd, 1 if ds == -1 else 0]
        elif ds == 0:
            src = SY.at[rnd]
            dst = RY.at[rnd, pl.ds(32, 256)]
        else:
            src = SY.at[rnd, pl.ds(0 if ds == -1 else 224, 32)]
            dst = RY.at[rnd, pl.ds(288 if ds == -1 else 0, 32)]
        return pltpu.make_async_remote_copy(
            src_ref=src, dst_ref=dst, send_sem=send_sem.at[rnd, k], recv_sem=recv_sem.at[rnd, k],
            device_id=target(dr, ds, dl), device_id_type=MESH,
        )

    def group(kind):
        dr, ds, dl = kind
        return "z" if dr else "x" if not dl else "edge" if ds else "y"

    def send(rnd, which):
        for k, (dr, ds, dl) in enumerate(KINDS):
            if group(KINDS[k]) in which:
                @pl.when(inside(dr, ds))
                def _(k=k):
                    message(rnd, k).start()

    def arrived(rnd, which):
        for k, (dr, ds, dl) in enumerate(KINDS):
            if group(KINDS[k]) in which:
                @pl.when(inside(-dr, -ds))
                def _(k=k):
                    message(rnd, k).wait_recv()

    def sent(rnd):
        for k, (dr, ds, dl) in enumerate(KINDS):
            @pl.when(inside(dr, ds))
            def _(k=k):
                message(rnd, k).wait_send()

    for load in loads[:4]:
        load.wait()
    lane128 = iota((8, 128), 1)
    slot = lane128 >> 3
    live = jnp.zeros((8, 128), F32)
    n_live = count[0, 0, 0]
    for k in range(bricks.shape[3]):
        entry = jnp.where(k < n_live, bricks[0, 0, 0, k], -1)
        live = jnp.where(slot == entry, 1.0, live)
    for x in range(8):
        ACT[x] = jnp.where(occ[x] == 1, live, 0.0)

    zl = iota((256, 128), 1)

    def shifted(v):
        before = jnp.where(zl[: v.shape[0]] == 0, 0.0, pltpu.roll(v, 1, 1))
        after = jnp.where(zl[: v.shape[0]] == 127, 0.0, pltpu.roll(v, 127, 1))
        return before.astype(BF), v.astype(BF), after.astype(BF)

    def places(x):
        got = []
        if -1 <= x <= 4:
            got.append((x + 1, 0))
        if 3 <= x <= 8:
            got.append((x - 3, 1))
        return got

    def put_plane(rnd, x, v):
        three = shifted(v)
        for p, h in places(x):
            for dz in range(3):
                D[rnd, p, dz, :, pl.ds(h * 128, 128)] = three[dz]
        if x == 0:
            SX[rnd, 0] = three[1]
        if x == 7:
            SX[rnd, 1] = three[1]

    ci = iota((32, 256), 0)
    cj = iota((32, 256), 1)
    spread = onehot(ci == (cj >> 3))
    pick_edge = onehot((ci == (cj >> 3)) & ((cj & 7) == edge))
    e_row = iota((16, 128), 0)
    e_lane = iota((16, 128), 1)

    def pack(rnd):
        columns = jnp.zeros((16, 256), F32)
        for x in range(8):
            p, h = places(x)[0]
            take = onehot(((e_row == x) & (e_lane == 0)) | ((e_row == 8 + x) & (e_lane == 127)))
            v = D[rnd, p, 1, :, pl.ds(h * 128, 128)]
            columns += dot_nt(take, v)
            SY[rnd, pl.ds(x * 32, 32)] = dot(pick_edge, v).astype(BF)
        SZ[rnd] = columns.astype(BF)

    def span(at, size):
        return 1 + jnp.where(at > 0, 1, 0) + jnp.where(at < size - 1, 1, 0)

    for x in (0, 7, 1, 2, 3, 4, 5, 6):
        v = feat[:, x].astype(F32) * ACT[x][None]
        put_plane(0, x, v.reshape(256, 128))
    pack(0)
    ri = iota((256, 256), 0)
    rj = iota((256, 256), 1)
    order = onehot((ri >> 3 == (rj & 31)) & ((ri & 7) == (rj >> 5)))
    bi = iota((256, 32), 0)
    bj = iota((256, 32), 1)
    put_edge = onehot(((bi >> 3) == bj) & ((bi & 7) == edge))
    band = [onehot((cj & 7) == k) for k in range(8)]
    far_band = onehot((cj & 7) == far)

    def build(layer, w):
        WC[...] = dot(w[...].reshape(27 * 32, 32), spread).astype(BF)
        for dx in range(3):
            for dz in range(3):
                taps = [WC[pl.ds((9 * dx + 3 * dy + dz) * 32, 32)] for dy in range(3)]
                blocks = []
                for y in range(8):
                    block = taps[1] * band[y]
                    if y > 0:
                        block = block + taps[0] * band[y - 1]
                    if y < 7:
                        block = block + taps[2] * band[y + 1]
                    blocks.append(block)
                full = jnp.concatenate(blocks, axis=0)
                B[layer, :, pl.ds((dx * 3 + dz) * 256, 256)] = dot(order, full).astype(BF)
                if dz != 1:
                    start = pl.multiple_of((9 * dx + 3 * (2 - 2 * l) + dz) * 32, 32)
                    BC[layer, dx * 2 + dz // 2] = dot(put_edge, WC[pl.ds(start, 32)] * far_band).astype(BF)
        side = jnp.zeros((32, 288), F32)
        pi = iota((32, 288), 0)
        pj = iota((32, 288), 1)
        for dx in range(3):
            for dz in range(3):
                tap = w[9 * dx + 3 * (2 - 2 * l) + dz]
                side += dot(tap, onehot(pj == pi + 32 * (dx * 3 + dz)))
        BY[layer] = dot(put_edge, side.astype(BF)).astype(BF)

    for load in loads[4:]:
        load.wait()
    build(0, w1)

    pl.semaphore_wait(barrier, span(r, n_region) * span(s, n_sub) * 2 - 1)
    send(0, ("z",))
    send(0, ("x",))
    send(0, ("edge", "y"))


    si = iota((96, 96), 0)
    sj = iota((96, 96), 1)
    q, j = si >> 4, si & 15
    plus = q & 1
    e = (j >> 1) + (q >> 1) + 7
    source = plus * 48 + (e >> 3) * 16 + (1 - plus) * 8 + (e & 7)
    place = onehot((sj == source) & ((j & 1) == 1 - plus))

    def rows_of(ref):
        own = jnp.broadcast_to(ref[...], (256, 32))
        return jnp.sum(jnp.where((bi >> 3) == bj, own, 0.0), axis=1, keepdims=True)

    G[...] = jnp.zeros_like(G)

    def main(layer, xx):
        return dot(B[layer], D[layer, pl.ds(xx, 3)].reshape(2304, 256))

    def put_rows(layer, x):
        three = shifted(RY[layer, pl.ds((x + 1) * 32, 32)].astype(F32))
        for p, h in places(x):
            for dz in range(3):
                DY[layer, pl.ds(p * 96 + dz * 32, 32), pl.ds(h * 128, 128)] = three[dz]

    def add_rows(layer, xx):
        ACC[xx] += dot(BY[layer], DY[layer, pl.ds(xx * 96, 288)])

    def layer_sums(layer):
        arrived(layer, ("y",))
        for x in range(8):
            put_rows(layer, x)
        add_rows(layer, 1)
        add_rows(layer, 2)
        arrived(layer, ("x",))
        for side, xx, first_row in ((0, 0, 0), (1, 3, 1536)):
            three = shifted(RX[layer, side].astype(F32))
            for dz in range(3):
                DX[side, dz] = three[dz]
            ACC[xx, :, pl.ds(side * 128, 128)] += dot(
                B[layer, :, pl.ds(first_row, 768)], DX[side].reshape(768, 128)
            )
        arrived(layer, ("edge",))
        put_rows(layer, -1)
        put_rows(layer, 8)
        add_rows(layer, 0)
        add_rows(layer, 3)
        arrived(layer, ("z",))
        own = dot(place, RZ[layer, 0]).astype(BF)
        other = dot(place, RZ[layer, 1]).astype(BF)
        total = jnp.zeros((256, 16), F32)
        for q in range(6):
            dx, dz = q // 2, 2 * (q % 2)
            total += dot_nt(B[layer, :, pl.ds((dx * 3 + dz) * 256, 256)], own[q * 16 : q * 16 + 16])
            total += dot_nt(BC[layer, q], other[q * 16 : q * 16 + 16])
        G[:, pl.ds(0, 16)] = total

    ends = (zl == 0) | (zl == 127)

    def finish(layer, xx, scale, shift):
        acc = ACC[xx]
        got = []
        for h in range(2):
            x = xx + 4 * h
            v = acc[:, h * 128 : h * 128 + 128]
            v = v + jnp.where(ends, pltpu.roll(G[...], 128 - (2 * x + 1), 1), 0.0)
            v = jnp.maximum(v * scale + shift, 0.0).reshape(32, 8, 128) * ACT[x][None]
            got.append((x, v))
        return got

    for xx in range(4):
        ACC[xx] = main(0, xx)
    build(1, w2)
    layer_sums(0)
    scale, shift = rows_of(s1), rows_of(h1)
    for xx in (0, 3, 1, 2):
        for x, v in finish(0, xx, scale, shift):
            put_plane(1, x, v.reshape(256, 128).astype(BF).astype(F32))
        if xx == 3:
            send(1, ("x",))
    pack(1)
    send(1, ("z",))
    send(1, ("edge", "y"))

    for xx in range(4):
        ACC[xx] = main(1, xx)
    layer_sums(1)
    scale, shift = rows_of(s2), rows_of(h2)
    for xx in (1, 2, 0, 3):
        for x, v in finish(1, xx, scale, shift):
            p, h = places(x)[0]
            begin = D[0, p, 1, :, pl.ds(h * 128, 128)].astype(F32).reshape(32, 8, 128)
            v = (v.astype(BF).astype(F32) + begin) * ACT[x][None]
            out[:, x] = v.astype(BF)
            pltpu.make_async_copy(out.at[:, x], out_hbm.at[:, x], out_sem.at[x]).start()
    sent(0)
    sent(1)
    for x in range(8):
        pltpu.make_async_copy(out.at[:, x], out_hbm.at[:, x], out_sem.at[x]).wait()


def body(n_region, n_sub, features, occupancy, brick_list, brick_count, w1, s1, h1, w2, s2, h2):
    assert features.shape == (32, 8, 8, 128)
    hbm = pl.BlockSpec(memory_space=pltpu.HBM)
    scales = [v.reshape(1, -1) for v in (s1, h1, s2, h2)]
    return pl.pallas_call(
        functools.partial(kernel, n_region, n_sub),
        out_shape=jax.ShapeDtypeStruct(features.shape, BF),
        in_specs=[hbm] * 10,
        out_specs=hbm,
        scratch_shapes=[
            pltpu.VMEM(features.shape, BF),
            pltpu.VMEM(occupancy.shape, jnp.int32),
            pltpu.SMEM(brick_list.shape, jnp.int32),
            pltpu.SMEM(brick_count.shape, jnp.int32),
            pltpu.VMEM(w1.shape, BF),
            pltpu.VMEM((1, 32), F32),
            pltpu.VMEM((1, 32), F32),
            pltpu.VMEM(w2.shape, BF),
            pltpu.VMEM((1, 32), F32),
            pltpu.VMEM((1, 32), F32),
            pltpu.SemaphoreType.DMA((10,)),
            pltpu.VMEM(features.shape, BF),
            pltpu.SemaphoreType.DMA((8,)),
            pltpu.VMEM((2, 3, 256, 128), BF),
            pltpu.VMEM((2, 6, 3, 256, 256), BF),
            pltpu.VMEM((2, 576, 256), BF),
            pltpu.VMEM((2, 256, 2304), BF),
            pltpu.VMEM((2, 256, 288), BF),
            pltpu.VMEM((2, 6, 256, 256), BF),
            pltpu.VMEM((864, 256), BF),
            pltpu.VMEM((4, 256, 256), F32),
            pltpu.VMEM((256, 128), F32),
            pltpu.VMEM((8, 8, 128), F32),
            pltpu.VMEM((2, 2, 256, 128), BF),
            pltpu.VMEM((2, 256, 128), BF),
            pltpu.VMEM((2, 16, 256), BF),
            pltpu.VMEM((2, 2, 256, 128), BF),
            pltpu.VMEM((2, 320, 128), BF),
            pltpu.VMEM((2, 2, 96, 256), BF),
            pltpu.SemaphoreType.DMA((2, len(KINDS))),
            pltpu.SemaphoreType.DMA((2, len(KINDS))),
        ],
        compiler_params=pltpu.CompilerParams(
            collective_id=0, has_side_effects=True, vmem_limit_bytes=64000 * 1024
        ),
    )(features, occupancy, brick_list, brick_count, w1, scales[0], scales[1], w2, scales[2], scales[3])


def solution(mesh):
    assert mesh.shape["lane"] == 2
    placed = (
        P(None, "sub", "lane", ("groups", "region")),
        P("sub", "lane", ("groups", "region")),
        P(("groups", "region"), "sub", "lane", None),
        P(("groups", "region"), "sub", "lane"),
        P(), P(), P(), P(), P(), P(),
    )
    return jax.shard_map(
        functools.partial(body, mesh.shape["region"], mesh.shape["sub"]),
        mesh=mesh,
        in_specs=placed,
        out_specs=P(None, "sub", "lane", ("groups", "region")),
        check_vma=False,
    )
```
